256 devices in a mesh: row: 32 (over x, y, core), col: 8 (over z).
Axes of the slice: x: 4, y: 4, z: 8, core: 2. Of those that a mesh axis runs over, the one named last changes fastest.
Arguments:
- source: bfloat16 [32768, 128], P(('row', 'col')), may hold values from -10 to 10
- target: bfloat16 [32768, 128], P(('col', 'row')), may hold values from -80 to 80
- target_potential: bfloat16 [32768], P(('col', 'row')), may hold values from -4 to 4
- prev_moment: float32 [128, 128], replicated, may hold values from -0.1 to 0.5
Outputs:
- moment: float32 [128, 128], replicated
- source_potential: float32 [32768], P('row')
- target_update: float32 [32768], P(('col', 'row'))
The draws below stay inside these ranges and needn't reach their ends.
All inputs are finite; a program needn't handle non-finite values.
Results may differ from the reference program's by a relative error of at most 0.0059.
Values may be sent and summed in bfloat16 or wider, within the bound.
A program may use at most 64 MiB of HBM per device.

```python
import math
import jax
import jax.numpy as jnp
from jax import lax

D = 128
ITERS = 2
NS = 32768
NT = 32768


def shared_parts(key):
    centres = jnp.clip(jax.random.normal(jax.random.fold_in(key, 101), (32, D), jnp.float32), -5.0, 5.0)
    return centres


def log_draw(key, shape, low, high):
    return jnp.exp(jax.random.uniform(key, shape, jnp.float32, math.log(low), math.log(high)))


def draw_source(key, part):
    centres = shared_parts(key)
    labels = jax.random.randint(jax.random.fold_in(key, 11), (NS,), 0, 32)
    noise = jnp.clip(jax.random.normal(jax.random.fold_in(key, 12), (NS, D), jnp.float32), -5.0, 5.0)
    base = 0.45 * (0.7071 * centres[labels] + 0.7071 * noise)
    return base.astype(jnp.bfloat16)


def draw_target(key, part):
    centres = shared_parts(key)
    labels = jax.random.randint(jax.random.fold_in(key, 21), (NT,), 0, 32)
    noise = jnp.clip(jax.random.normal(jax.random.fold_in(key, 22), (NT, D), jnp.float32), -5.0, 5.0)
    base = 0.45 * (0.7071 * centres[labels] + 0.7071 * noise)
    return base.astype(jnp.bfloat16)


def draw_prev_moment(key, part):
    diag_values = 0.25 * log_draw(jax.random.fold_in(key, 41), (D,), 0.6, 1.6)
    noise = 0.015 * jnp.clip(jax.random.normal(jax.random.fold_in(key, 42), (D, D), jnp.float32), -4.0, 4.0)
    places = jnp.arange(D)
    on_diag = places[:, None] == places[None, :]
    return jnp.where(on_diag, diag_values[None, :], 0.0) + noise


def block_scale(stream_key, shape, split, smallest, high):
    def one(axis_at, shards_of):
        heights = jax.random.uniform(jax.random.fold_in(jax.random.fold_in(stream_key, 6), axis_at), (shards_of,), jnp.float32, smallest / len(split), high / len(split))
        return jnp.repeat(jnp.exp(heights), shape[axis_at] // shards_of).reshape((-1,) + (1,) * (len(shape) - axis_at - 1))

    loudness = one(*split[0])
    for cut in split[1:]:
        loudness = loudness * one(*cut)
    return loudness


def normal_values(stream_key, extent, width, reach, pieces=(), dtype=jnp.bfloat16):
    result = jax.random.normal(stream_key, extent, jnp.float32) * width
    if len(pieces) > 0:
        result = block_scale(stream_key, extent, pieces, -0.22, 0.18) * result
    return jnp.clip(result, min=-reach, max=reach).astype(dtype)


def setup_inputs(seed: int = 0) -> dict:
    keys = jax.random.split(jax.random.key(seed), 5)
    source = draw_source(jax.random.fold_in(keys[4], 71), 0)
    target = draw_target(jax.random.fold_in(keys[4], 71), 0)
    target_potential = normal_values(keys[2], (NT,), 1.0, 4.0, ((0, 256),))
    prev_moment = draw_prev_moment(jax.random.fold_in(keys[4], 71), 0)
    return dict(source=source, target=target, target_potential=target_potential, prev_moment=prev_moment)


def project(rows, matrix):
    return jnp.dot(rows.astype(jnp.float32), matrix.astype(jnp.float32), precision=lax.Precision.HIGHEST).astype(jnp.bfloat16)


def tile_costs(projected, target):
    return -4.0 * jnp.dot(projected, target.T, preferred_element_type=jnp.float32)


def log_totals(scores, axis):
    top_score = jnp.max(scores, axis=axis, keepdims=True)
    return jnp.squeeze(top_score, axis) + jnp.log(jnp.sum(jnp.exp(scores - top_score), axis=axis))


def reference(source, target, target_potential, prev_moment):
    block_rows = min(512, NS)
    blocks = source.reshape(NS // block_rows, block_rows, D)
    column = target_potential.astype(jnp.float32)

    def couple(total, rows):
        scores = column[None, :] - tile_costs(project(rows, prev_moment), target)
        spread = log_totals(scores, 1)
        weights = (jnp.exp(scores - spread[:, None]) / NS).astype(jnp.bfloat16)
        carried = jnp.dot(weights, target, preferred_element_type=jnp.float32)
        return total + jnp.dot(rows.astype(jnp.float32).T, carried, precision=lax.Precision.HIGHEST), None

    moment, _ = lax.scan(couple, jnp.zeros((D, D), jnp.float32), blocks)

    def column_step(carry, item):
        rows, potential = item
        top_score, mass_total = carry
        scores = potential[:, None] - tile_costs(project(rows, moment), target)
        new_top = jnp.maximum(top_score, jnp.max(scores, axis=0))
        mass_total = mass_total * jnp.exp(top_score - new_top) + jnp.sum(jnp.exp(scores - new_top[None, :]), axis=0)
        return (new_top, mass_total), None

    source_potential = jnp.zeros((NS // block_rows, block_rows), jnp.float32)
    for iteration in range(ITERS):
        current = column
        source_potential = lax.map(lambda rows: math.log(NT) - log_totals(current[None, :] - tile_costs(project(rows, moment), target), 1), blocks)
        start = (jnp.full((NT,), -jnp.inf, jnp.float32), jnp.zeros((NT,), jnp.float32))
        (top_score, mass_total), _ = lax.scan(column_step, start, (blocks, source_potential))
        column = math.log(NS) - (top_score + jnp.log(mass_total))
    return moment, source_potential.reshape(NS), column
```

```python
import math

import jax
import jax.numpy as jnp
from jax import lax
from jax.experimental import pallas as pl
from jax.experimental.pallas import tpu as pltpu
from jax.sharding import PartitionSpec as P

MESH = pl.DeviceIdType.MESH
F32, BF16 = jnp.float32, jnp.bfloat16
D = 128
ROWS = 32
COLS = 8
NR = 1024
NC = 4096
N = 32768
LOG_N = math.log(N)
PAD = 144
TC = 512
RC = 256
CC = 512

NT_DIMS = (((1,), (1,)), ((), ()))
TN_DIMS = (((0,), (0,)), ((), ()))


def split3(value):
    high = value.astype(BF16)
    rest = value - high.astype(F32)
    middle = rest.astype(BF16)
    return high, middle, (rest - middle.astype(F32)).astype(BF16)


def dot_nt(a, b):
    return lax.dot_general(a, b, NT_DIMS, preferred_element_type=F32)


def dot_nn(a, b):
    return jnp.dot(a, b, preferred_element_type=F32)


def kernel(
    source_ref, target_ref, potential_ref, prev_ref,
    moment_ref, row_out_ref, col_out_ref,
    src, tbuf, taug, paug, tile, kernel_tile, frep, chunk_top, col_top, col_mass,
    stage_row, row_in1, row_in2, row_in3,
    mom_stage, mom_in, own_mom, mom_z, mom_all,
    stage_col, col_in, col_in2, col_all, own_col,
    src_send, src_recv, t_send, t_recv, f_send,
    send_sem, recv_sem,
):
    me_r = lax.axis_index("row")
    me_z = lax.axis_index("col")
    core = lax.rem(me_r, 2)
    chip = lax.div(me_r, 2)
    sibling = chip * 2 + (1 - core)

    def row_peer(k):
        return lax.rem(me_r + k, ROWS)

    def z_peer(k):
        return lax.rem(me_z + k, COLS)

    def plane_peer(k):
        return lax.rem(chip + k, ROWS // 2) * 2 + core

    def remote(source, dest, send, recv, row, col):
        return pltpu.make_async_remote_copy(
            src_ref=source, dst_ref=dest, send_sem=send, recv_sem=recv,
            device_id=(row, col), device_id_type=MESH,
        )

    def settle(buffer, sem):
        pltpu.make_async_copy(buffer, buffer, sem).wait()

    barrier = pltpu.get_barrier_semaphore()

    def greet_row(k, _):
        pl.semaphore_signal(barrier, inc=1, device_id=(row_peer(k), me_z), device_id_type=MESH)
        return _

    def greet_z(k, _):
        pl.semaphore_signal(barrier, inc=1, device_id=(me_r, z_peer(k)), device_id_type=MESH)
        return _

    lax.fori_loop(1, ROWS, greet_row, 0)
    lax.fori_loop(1, COLS, greet_z, 0)
    src[me_z] = source_ref[...]
    tbuf[me_r, 0:D] = target_ref[...]
    tbuf[me_r, D:PAD] = jnp.broadcast_to(potential_ref[...], (PAD - D, D)).astype(BF16)
    paug[:, D:] = jnp.ones((NR, D), BF16)
    pl.semaphore_wait(barrier, ROWS + COLS - 2)

    def send_source(k, _):
        remote(src.at[me_z], src.at[me_z], src_send, src_recv, me_r, z_peer(k)).start()
        return _

    def send_target(k, _):
        remote(tbuf.at[me_r], tbuf.at[me_r], t_send, t_recv.at[me_r], plane_peer(k), me_z).start()
        return _

    remote(tbuf.at[me_r], tbuf.at[me_r], f_send, t_recv.at[me_r], sibling, me_z).start()
    lax.fori_loop(1, COLS, send_source, 0)
    lax.fori_loop(1, ROWS // 2, send_target, 0)

    def forward(k, _):
        slot = plane_peer(k)
        settle(tbuf.at[slot], t_recv.at[slot])
        remote(tbuf.at[slot], tbuf.at[slot], f_send, t_recv.at[slot], sibling, me_z).start()
        return _

    lax.fori_loop(1, ROWS // 2, forward, 0)

    settle(src.at[pl.ds(0, COLS - 1)], src_recv)
    settle(src.at[pl.ds(0, COLS - 1)], src_send)

    def project(parts):
        rows = src[...].reshape(NR, D)
        total = parts(rows)
        paug[:, 0:D] = (4.0 * total).astype(BF16)

    def project_prev(rows):
        high, middle, low = split3(prev_ref[...])
        return dot_nn(rows, high) + (dot_nn(rows, middle) + dot_nn(rows, low))

    project(project_prev)

    def arrive(k, _):
        slot = lax.rem(chip + k, ROWS // 2) * 2 + (1 - core)
        settle(tbuf.at[slot], t_recv.at[slot])
        return _

    lax.fori_loop(0, ROWS // 2, arrive, 0)
    settle(tbuf.at[pl.ds(0, ROWS // 2 - 1)], t_send)
    settle(tbuf.at[pl.ds(0, ROWS // 2)], f_send)

    eye = lax.broadcasted_iota(jnp.int32, (D, D), 0) == lax.broadcasted_iota(jnp.int32, (D, D), 1)

    def place(k, _):
        block = tbuf[k]
        at = pl.ds(pl.multiple_of(k * D, D), D)
        taug[at, 0:D] = block[0:D]
        taug[at, D:] = jnp.where(eye, block[D : D + 1].astype(F32), 0.0).astype(BF16)
        return _

    lax.fori_loop(0, ROWS, place, 0)

    def row_pass(keep):
        def step(c, carry):
            top, mass = carry
            at = pl.ds(pl.multiple_of(c * TC, TC), TC)
            scores = dot_nt(taug[at, :], paug[...])
            here = jnp.max(scores, axis=0, keepdims=True)
            weights = jnp.exp(scores - here)
            if keep:
                tile[at, :] = weights.astype(BF16)
                chunk_top[c] = here
            new_top = jnp.maximum(top, here)
            mass = mass * jnp.exp(top - new_top) + jnp.sum(weights, axis=0, keepdims=True) * jnp.exp(here - new_top)
            return new_top, mass

        start = (jnp.full((1, NR), -jnp.inf, F32), jnp.zeros((1, NR), F32))
        return lax.fori_loop(0, NC // TC, step, start)

    def send_z(stage, inbox, channel):
        def one(k, _):
            remote(stage, inbox.at[me_z], send_sem.at[channel], recv_sem.at[channel], me_r, z_peer(k)).start()
            return _

        lax.fori_loop(1, COLS, one, 0)
        inbox[me_z] = stage[...]

    def wait_z(inbox, channel):
        settle(inbox.at[pl.ds(0, COLS - 1)], recv_sem.at[channel])
        settle(inbox.at[pl.ds(0, COLS - 1)], send_sem.at[channel])

    def total_lse(inbox):
        values = inbox[...]
        top = jnp.max(values, axis=0)
        return top + jnp.log(jnp.sum(jnp.exp(values - top[None]), axis=0))

    top, mass = row_pass(True)
    stage_row[...] = top + jnp.log(mass)
    send_z(stage_row, row_in1, 0)

    def carry_step(c, total):
        at = pl.ds(pl.multiple_of(c * TC, TC), TC)
        part = lax.dot_general(taug[at, 0:D], tile[at, :], TN_DIMS, preferred_element_type=F32)
        return total + part * jnp.exp(chunk_top[c] - top)

    carried = lax.fori_loop(0, NC // TC, carry_step, jnp.zeros((D, NR), F32))
    wait_z(row_in1, 0)
    carried = carried * (jnp.exp(top - total_lse(row_in1)) / N)
    rows = src[...].reshape(NR, D)
    high, middle, low = split3(carried)
    part_moment = dot_nn(high, rows) + (dot_nn(middle, rows) + dot_nn(low, rows))
    for k in range(ROWS):
        mom_stage[k] = part_moment[4 * k : 4 * k + 4]

    def send_moment(k, _):
        peer = row_peer(k)
        remote(mom_stage.at[peer], mom_in.at[me_r], send_sem.at[1], recv_sem.at[1], peer, me_z).start()
        return _

    lax.fori_loop(1, ROWS, send_moment, 0)
    mom_in[me_r] = mom_stage[me_r]
    settle(mom_in.at[pl.ds(0, ROWS - 1)], recv_sem.at[1])
    settle(mom_in.at[pl.ds(0, ROWS - 1)], send_sem.at[1])
    own_mom[0] = jnp.sum(mom_in[...], axis=0)
    send_z(own_mom.at[0], mom_z, 2)
    wait_z(mom_z, 2)
    own_mom[1] = jnp.sum(mom_z[...], axis=0)

    def share_moment(k, _):
        remote(own_mom.at[1], mom_all.at[me_r], send_sem.at[3], recv_sem.at[3], row_peer(k), me_z).start()
        return _

    lax.fori_loop(1, ROWS, share_moment, 0)
    mom_all[me_r] = own_mom[1]
    settle(mom_all.at[pl.ds(0, ROWS - 1)], recv_sem.at[3])
    settle(mom_all.at[pl.ds(0, ROWS - 1)], send_sem.at[3])
    for k in range(ROWS):
        moment_ref[4 * k : 4 * k + 4, :] = mom_all[k]
    moment_t = moment_ref[...]

    def project_new(block):
        first, second, third = split3(moment_t)
        return dot_nt(block, first) + (dot_nt(block, second) + dot_nt(block, third))

    project(project_new)
    moment_ref[...] = moment_t.T

    top, mass = row_pass(False)
    stage_row[...] = top + jnp.log(mass)
    send_z(stage_row, row_in2, 4)
    wait_z(row_in2, 4)
    first_row = LOG_N - total_lse(row_in2)

    for k in range(NR // D):
        frep[k * D : (k + 1) * D, :] = jnp.broadcast_to(first_row[:, k * D : (k + 1) * D], (D, D)).T

    def col_step(step, _):
        r = lax.div(step, NC // CC)
        c = lax.rem(step, NC // CC)
        rows_at = pl.ds(pl.multiple_of(r * RC, RC), RC)
        cols_at = pl.ds(pl.multiple_of(c * CC, CC), CC)
        shift = frep[rows_at, :]
        scores = dot_nt(paug[rows_at, 0:D], taug[cols_at, 0:D]) + jnp.concatenate([shift] * (CC // D), axis=1)
        here = jnp.max(scores, axis=0, keepdims=True)
        weights = jnp.exp(scores - here)
        kernel_tile[rows_at, cols_at] = weights.astype(BF16)
        col_top[r, :, cols_at] = here
        col_mass[r, :, cols_at] = jnp.sum(weights, axis=0, keepdims=True)
        return _

    lax.fori_loop(0, (NR // RC) * (NC // CC), col_step, 0)
    tops = col_top[...]
    best = jnp.max(tops, axis=0)
    stage_col[0] = best + jnp.log(jnp.sum(col_mass[...] * jnp.exp(tops - best[None]), axis=0))

    def lanes(k):
        return pl.ds(pl.multiple_of(k * D, D), D)

    def scatter_cols(index, inbox, channel):
        def one(k, _):
            peer = row_peer(k)
            remote(
                stage_col.at[index, :, lanes(peer)], inbox.at[me_r],
                send_sem.at[channel], recv_sem.at[channel], peer, me_z,
            ).start()
            return _

        lax.fori_loop(1, ROWS, one, 0)
        inbox[me_r] = stage_col[index, :, lanes(me_r)]
        settle(inbox.at[pl.ds(0, ROWS - 1)], recv_sem.at[channel])
        settle(inbox.at[pl.ds(0, ROWS - 1)], send_sem.at[channel])

    scatter_cols(0, col_in, 5)
    own_col[...] = LOG_N - total_lse(col_in)

    def share_col(k, _):
        remote(own_col, col_all.at[:, lanes(me_r)], send_sem.at[6], recv_sem.at[6], row_peer(k), me_z).start()
        return _

    lax.fori_loop(1, ROWS, share_col, 0)
    col_all[:, lanes(me_r)] = own_col[...]
    settle(col_all.at[:, pl.ds(0, NC - D)], recv_sem.at[6])
    settle(col_all.at[:, pl.ds(0, NC - D)], send_sem.at[6])

    first_col = col_all[...]
    line = lax.broadcasted_iota(jnp.int32, (16, 1), 0)
    lhs = jnp.zeros((16, NC), F32)
    for r in range(NR // RC):
        factor = jnp.exp(first_col + col_top[r])
        col_mass[r] = factor
        for p, piece in enumerate(split3(factor)):
            lhs = jnp.where(line == 3 * r + p, piece.astype(F32), lhs)
    sums = dot_nt(lhs.astype(BF16), kernel_tile[...])
    for r in range(NR // RC):
        at = slice(r * RC, (r + 1) * RC)
        stage_row[:, at] = (
            sums[3 * r : 3 * r + 1, at] + (sums[3 * r + 1 : 3 * r + 2, at] + sums[3 * r + 2 : 3 * r + 3, at])
        )
    send_z(stage_row, row_in3, 7)
    wait_z(row_in3, 7)
    row_sum = jnp.sum(row_in3[...], axis=0)
    row_out_ref[...] = first_row + (LOG_N - jnp.log(row_sum))
    high, middle, low = split3(N / row_sum)
    scale = jnp.where(
        line == 0, high.astype(F32), jnp.where(line == 1, middle.astype(F32), jnp.where(line == 2, low.astype(F32), 0.0))
    ).astype(BF16)
    total = jnp.zeros((1, NC), F32)
    for r in range(NR // RC):
        at = slice(r * RC, (r + 1) * RC)
        part = dot_nn(scale[:, at], kernel_tile[at, :])
        total = total + (part[0:1] + (part[1:2] + part[2:3])) * col_mass[r]
    stage_col[1] = total
    scatter_cols(1, col_in2, 8)
    col_out_ref[...] = own_col[...] + (LOG_N - jnp.log(jnp.sum(col_in2[...], axis=0)))


def per_device(source, target, target_potential, prev_moment):
    vmem = pl.BlockSpec(memory_space=pltpu.VMEM)
    dma = pltpu.SemaphoreType.DMA
    moment, row, col = pl.pallas_call(
        kernel,
        out_shape=(
            jax.ShapeDtypeStruct((D, D), F32),
            jax.ShapeDtypeStruct((1, NR), F32),
            jax.ShapeDtypeStruct((1, D), F32),
        ),
        in_specs=[vmem] * 4,
        out_specs=(vmem,) * 3,
        scratch_shapes=[
            pltpu.VMEM((COLS, D, D), BF16),
            pltpu.VMEM((ROWS, PAD, D), BF16),
            pltpu.VMEM((NC, 2 * D), BF16),
            pltpu.VMEM((NR, 2 * D), BF16),
            pltpu.VMEM((NC, NR), BF16),
            pltpu.VMEM((NR, NC), BF16),
            pltpu.VMEM((NR, D), F32),
            pltpu.VMEM((NC // TC, 1, NR), F32),
            pltpu.VMEM((NR // RC, 1, NC), F32),
            pltpu.VMEM((NR // RC, 1, NC), F32),
            pltpu.VMEM((1, NR), F32),
            pltpu.VMEM((COLS, 1, NR), F32),
            pltpu.VMEM((COLS, 1, NR), F32),
            pltpu.VMEM((COLS, 1, NR), F32),
            pltpu.VMEM((ROWS, 4, D), F32),
            pltpu.VMEM((ROWS, 4, D), F32),
            pltpu.VMEM((2, 4, D), F32),
            pltpu.VMEM((COLS, 4, D), F32),
            pltpu.VMEM((ROWS, 4, D), F32),
            pltpu.VMEM((2, 1, NC), F32),
            pltpu.VMEM((ROWS, 1, D), F32),
            pltpu.VMEM((ROWS, 1, D), F32),
            pltpu.VMEM((1, NC), F32),
            pltpu.VMEM((1, D), F32),
            dma, dma, dma, dma((ROWS,)), dma,
            dma((9,)), dma((9,)),
        ],
        compiler_params=pltpu.CompilerParams(
            collective_id=0, has_side_effects=True, vmem_limit_bytes=58 << 20
        ),
    )(source, target, target_potential.astype(F32).reshape(1, D), prev_moment)
    return moment, row.reshape(NR), col.reshape(D)


def solution(mesh):
    placed = (P(("row", "col"), None), P(("col", "row"), None), P(("col", "row")), P())
    return jax.shard_map(
        per_device,
        mesh=mesh,
        in_specs=placed,
        out_specs=(P(), P("row"), P(("col", "row"))),
        check_vma=False,
    )
```

```python
import math

import jax
import jax.numpy as jnp
from jax import lax
from jax.experimental import pallas as pl
from jax.experimental.pallas import tpu as pltpu
from jax.sharding import PartitionSpec as P

MESH = pl.DeviceIdType.MESH
F32, BF16 = jnp.float32, jnp.bfloat16
D = 128
ROWS = 32
COLS = 8
NR = 1024
NC = 4096
N = 32768
LOG_N = math.log(N)
PAD = 144
TC = NC
RC = NR
CC = NC

NT_DIMS = (((1,), (1,)), ((), ()))
TN_DIMS = (((0,), (0,)), ((), ()))


def split3(value):
    high = value.astype(BF16)
    rest = value - high.astype(F32)
    middle = rest.astype(BF16)
    return high, middle, (rest - middle.astype(F32)).astype(BF16)


def dot_nt(a, b):
    return lax.dot_general(a, b, NT_DIMS, preferred_element_type=F32)


def dot_nn(a, b):
    return jnp.dot(a, b, preferred_element_type=F32)


def kernel(
    source_ref, target_ref, potential_ref, prev_ref,
    moment_ref, row_out_ref, col_out_ref,
    src, tbuf, taug, paug, tile, kernel_tile, frep, chunk_top, col_top, col_mass,
    stage_row, row_in1, row_in2, row_in3,
    mom_stage, mom_in, own_mom, mom_z, mom_all,
    stage_col, col_in, col_in2, col_all, own_col,
    src_send, src_recv, t_send, t_recv, f_send,
    send_sem, recv_sem,
):
    me_r = lax.axis_index("row")
    me_z = lax.axis_index("col")
    core = lax.rem(me_r, 2)
    chip = lax.div(me_r, 2)
    sibling = chip * 2 + (1 - core)

    def row_peer(k):
        return lax.rem(me_r + k, ROWS)

    def z_peer(k):
        return lax.rem(me_z + k, COLS)

    def plane_peer(k):
        return lax.rem(chip + k, ROWS // 2) * 2 + core

    def remote(source, dest, send, recv, row, col):
        return pltpu.make_async_remote_copy(
            src_ref=source, dst_ref=dest, send_sem=send, recv_sem=recv,
            device_id=(row, col), device_id_type=MESH,
        )

    def settle(buffer, sem):
        pltpu.make_async_copy(buffer, buffer, sem).wait()

    barrier = pltpu.get_barrier_semaphore()

    def greet_row(k, _):
        pl.semaphore_signal(barrier, inc=1, device_id=(row_peer(k), me_z), device_id_type=MESH)
        return _

    def greet_z(k, _):
        pl.semaphore_signal(barrier, inc=1, device_id=(me_r, z_peer(k)), device_id_type=MESH)
        return _

    lax.fori_loop(1, ROWS, greet_row, 0)
    lax.fori_loop(1, COLS, greet_z, 0)
    src[me_z] = source_ref[...]
    tbuf[me_r, 0:D] = target_ref[...]
    tbuf[me_r, D:PAD] = jnp.broadcast_to(potential_ref[...].astype(F32).reshape(1, D), (PAD - D, D)).astype(BF16)
    paug[:, D:] = jnp.ones((NR, D), BF16)
    pl.semaphore_wait(barrier, ROWS + COLS - 2)

    def send_source(k, _):
        remote(src.at[me_z], src.at[me_z], src_send, src_recv, me_r, z_peer(k)).start()
        return _

    def send_target(k, _):
        remote(tbuf.at[me_r], tbuf.at[me_r], t_send, t_recv.at[me_r], plane_peer(k), me_z).start()
        return _

    remote(tbuf.at[me_r], tbuf.at[me_r], f_send, t_recv.at[me_r], sibling, me_z).start()
    lax.fori_loop(1, COLS, send_source, 0)
    lax.fori_loop(1, ROWS // 2, send_target, 0)

    def forward(k, _):
        slot = plane_peer(k)
        settle(tbuf.at[slot], t_recv.at[slot])
        remote(tbuf.at[slot], tbuf.at[slot], f_send, t_recv.at[slot], sibling, me_z).start()
        return _

    lax.fori_loop(1, ROWS // 2, forward, 0)

    settle(src.at[pl.ds(0, COLS - 1)], src_recv)
    settle(src.at[pl.ds(0, COLS - 1)], src_send)

    def project(parts):
        rows = src[...].reshape(NR, D)
        total = parts(rows)
        paug[:, 0:D] = (4.0 * total).astype(BF16)

    def project_prev(rows):
        high, middle, low = split3(prev_ref[...])
        return dot_nn(rows, high) + (dot_nn(rows, middle) + dot_nn(rows, low))

    project(project_prev)

    def arrive(k, _):
        slot = lax.rem(chip + k, ROWS // 2) * 2 + (1 - core)
        settle(tbuf.at[slot], t_recv.at[slot])
        return _

    lax.fori_loop(0, ROWS // 2, arrive, 0)
    settle(tbuf.at[pl.ds(0, ROWS // 2 - 1)], t_send)
    settle(tbuf.at[pl.ds(0, ROWS // 2)], f_send)

    eye = lax.broadcasted_iota(jnp.int32, (D, D), 0) == lax.broadcasted_iota(jnp.int32, (D, D), 1)

    def place(k, _):
        block = tbuf[k]
        at = pl.ds(pl.multiple_of(k * D, D), D)
        taug[at, 0:D] = block[0:D]
        taug[at, D:] = jnp.where(eye, block[D : D + 1].astype(F32), 0.0).astype(BF16)
        return _

    lax.fori_loop(0, ROWS, place, 0)

    def row_pass(keep):
        def step(c, carry):
            top, mass = carry
            at = pl.ds(pl.multiple_of(c * TC, TC), TC)
            scores = dot_nt(taug[at, :], paug[...])
            here = jnp.max(scores, axis=0, keepdims=True)
            weights = jnp.exp(scores - here)
            if keep:
                tile[at, :] = weights.astype(BF16)
                chunk_top[c] = here
            new_top = jnp.maximum(top, here)
            mass = mass * jnp.exp(top - new_top) + jnp.sum(weights, axis=0, keepdims=True) * jnp.exp(here - new_top)
            return new_top, mass

        start = (jnp.full((1, NR), -jnp.inf, F32), jnp.zeros((1, NR), F32))
        return lax.fori_loop(0, NC // TC, step, start)

    def send_z(stage, inbox, channel):
        def one(k, _):
            remote(stage, inbox.at[me_z], send_sem.at[channel], recv_sem.at[channel], me_r, z_peer(k)).start()
            return _

        lax.fori_loop(1, COLS, one, 0)
        inbox[me_z] = stage[...]

    def wait_z(inbox, channel):
        settle(inbox.at[pl.ds(0, COLS - 1)], recv_sem.at[channel])
        settle(inbox.at[pl.ds(0, COLS - 1)], send_sem.at[channel])

    def total_lse(inbox):
        values = inbox[...]
        top = jnp.max(values, axis=0)
        return top + jnp.log(jnp.sum(jnp.exp(values - top[None]), axis=0))

    top, mass = row_pass(True)
    stage_row[...] = top + jnp.log(mass)
    send_z(stage_row, row_in1, 0)

    def carry_step(c, total):
        at = pl.ds(pl.multiple_of(c * TC, TC), TC)
        part = lax.dot_general(taug[at, 0:D], tile[at, :], TN_DIMS, preferred_element_type=F32)
        return total + part * jnp.exp(chunk_top[c] - top)

    carried = lax.fori_loop(0, NC // TC, carry_step, jnp.zeros((D, NR), F32))
    wait_z(row_in1, 0)
    carried = carried * (jnp.exp(top - total_lse(row_in1)) / N)
    rows = src[...].reshape(NR, D)
    high, middle, low = split3(carried)
    part_moment = dot_nn(high, rows) + (dot_nn(middle, rows) + dot_nn(low, rows))
    for k in range(ROWS):
        mom_stage[k] = part_moment[4 * k : 4 * k + 4]

    def send_moment(k, _):
        peer = row_peer(k)
        remote(mom_stage.at[peer], mom_in.at[me_r], send_sem.at[1], recv_sem.at[1], peer, me_z).start()
        return _

    lax.fori_loop(1, ROWS, send_moment, 0)
    mom_in[me_r] = mom_stage[me_r]
    settle(mom_in.at[pl.ds(0, ROWS - 1)], recv_sem.at[1])
    settle(mom_in.at[pl.ds(0, ROWS - 1)], send_sem.at[1])
    own_mom[0] = jnp.sum(mom_in[...], axis=0)
    send_z(own_mom.at[0], mom_z, 2)
    wait_z(mom_z, 2)
    own_mom[1] = jnp.sum(mom_z[...], axis=0)

    def share_moment(k, _):
        remote(own_mom.at[1], mom_all.at[me_r], send_sem.at[3], recv_sem.at[3], row_peer(k), me_z).start()
        return _

    lax.fori_loop(1, ROWS, share_moment, 0)
    mom_all[me_r] = own_mom[1]
    settle(mom_all.at[pl.ds(0, ROWS - 1)], recv_sem.at[3])
    settle(mom_all.at[pl.ds(0, ROWS - 1)], send_sem.at[3])
    for k in range(ROWS):
        moment_ref[4 * k : 4 * k + 4, :] = mom_all[k]
    moment_t = moment_ref[...]

    def project_new(block):
        first, second, third = split3(moment_t)
        return dot_nt(block, first) + (dot_nt(block, second) + dot_nt(block, third))

    project(project_new)
    moment_ref[...] = moment_t.T

    top, mass = row_pass(False)
    stage_row[...] = top + jnp.log(mass)
    send_z(stage_row, row_in2, 4)
    wait_z(row_in2, 4)
    first_row = LOG_N - total_lse(row_in2)

    for k in range(NR // D):
        frep[k * D : (k + 1) * D, :] = jnp.broadcast_to(first_row[:, k * D : (k + 1) * D], (D, D)).T

    def col_step(step, _):
        r = lax.div(step, NC // CC)
        c = lax.rem(step, NC // CC)
        rows_at = pl.ds(pl.multiple_of(r * RC, RC), RC)
        cols_at = pl.ds(pl.multiple_of(c * CC, CC), CC)
        shift = frep[rows_at, :]
        scores = dot_nt(paug[rows_at, 0:D], taug[cols_at, 0:D]) + jnp.concatenate([shift] * (CC // D), axis=1)
        here = jnp.max(scores, axis=0, keepdims=True)
        weights = jnp.exp(scores - here)
        kernel_tile[rows_at, cols_at] = weights.astype(BF16)
        col_top[r, :, cols_at] = here
        col_mass[r, :, cols_at] = jnp.sum(weights, axis=0, keepdims=True)
        return _

    lax.fori_loop(0, (NR // RC) * (NC // CC), col_step, 0)
    tops = col_top[...]
    best = jnp.max(tops, axis=0)
    stage_col[0] = best + jnp.log(jnp.sum(col_mass[...] * jnp.exp(tops - best[None]), axis=0))

    def lanes(k):
        return pl.ds(pl.multiple_of(k * D, D), D)

    def scatter_cols(index, inbox, channel):
        def one(k, _):
            peer = row_peer(k)
            remote(
                stage_col.at[index, :, lanes(peer)], inbox.at[me_r],
                send_sem.at[channel], recv_sem.at[channel], peer, me_z,
            ).start()
            return _

        lax.fori_loop(1, ROWS, one, 0)
        inbox[me_r] = stage_col[index, :, lanes(me_r)]
        settle(inbox.at[pl.ds(0, ROWS - 1)], recv_sem.at[channel])
        settle(inbox.at[pl.ds(0, ROWS - 1)], send_sem.at[channel])

    scatter_cols(0, col_in, 5)
    own_col[...] = LOG_N - total_lse(col_in)

    def share_col(k, _):
        remote(own_col, col_all.at[:, lanes(me_r)], send_sem.at[6], recv_sem.at[6], row_peer(k), me_z).start()
        return _

    lax.fori_loop(1, ROWS, share_col, 0)
    col_all[:, lanes(me_r)] = own_col[...]
    settle(col_all.at[:, pl.ds(0, NC - D)], recv_sem.at[6])
    settle(col_all.at[:, pl.ds(0, NC - D)], send_sem.at[6])

    first_col = col_all[...]
    line = lax.broadcasted_iota(jnp.int32, (16, 1), 0)
    lhs = jnp.zeros((16, NC), F32)
    for r in range(NR // RC):
        factor = jnp.exp(first_col + col_top[r])
        col_mass[r] = factor
        for p, piece in enumerate(split3(factor)):
            lhs = jnp.where(line == 3 * r + p, piece.astype(F32), lhs)
    sums = dot_nt(lhs.astype(BF16), kernel_tile[...])
    for r in range(NR // RC):
        at = slice(r * RC, (r + 1) * RC)
        stage_row[:, at] = (
            sums[3 * r : 3 * r + 1, at] + (sums[3 * r + 1 : 3 * r + 2, at] + sums[3 * r + 2 : 3 * r + 3, at])
        )
    send_z(stage_row, row_in3, 7)
    wait_z(row_in3, 7)
    row_sum = jnp.sum(row_in3[...], axis=0)
    row_out_ref[...] = first_row + (LOG_N - jnp.log(row_sum))
    high, middle, low = split3(N / row_sum)
    scale = jnp.where(
        line == 0, high.astype(F32), jnp.where(line == 1, middle.astype(F32), jnp.where(line == 2, low.astype(F32), 0.0))
    ).astype(BF16)
    total = jnp.zeros((1, NC), F32)
    for r in range(NR // RC):
        at = slice(r * RC, (r + 1) * RC)
        part = dot_nn(scale[:, at], kernel_tile[at, :])
        total = total + (part[0:1] + (part[1:2] + part[2:3])) * col_mass[r]
    stage_col[1] = total
    scatter_cols(1, col_in2, 8)
    col_out_ref[...] = own_col[...] + (LOG_N - jnp.log(jnp.sum(col_in2[...], axis=0)))


def hand_over(moment_ref, row_ref, col_ref, moment_out, row_out, col_out):
    moment_out[...] = moment_ref[...]
    row_out[...] = row_ref[...].reshape(NR)
    col_out[...] = col_ref[...].reshape(D)


def per_device(source, target, target_potential, prev_moment):
    vmem = pl.BlockSpec(memory_space=pltpu.VMEM)
    dma = pltpu.SemaphoreType.DMA
    moment, row, col = pl.pallas_call(
        kernel,
        out_shape=(
            jax.ShapeDtypeStruct((D, D), F32),
            jax.ShapeDtypeStruct((1, NR), F32),
            jax.ShapeDtypeStruct((1, D), F32),
        ),
        in_specs=[vmem] * 4,
        out_specs=(vmem,) * 3,
        scratch_shapes=[
            pltpu.VMEM((COLS, D, D), BF16),
            pltpu.VMEM((ROWS, PAD, D), BF16),
            pltpu.VMEM((NC, 2 * D), BF16),
            pltpu.VMEM((NR, 2 * D), BF16),
            pltpu.VMEM((NC, NR), BF16),
            pltpu.VMEM((NR, NC), BF16),
            pltpu.VMEM((NR, D), F32),
            pltpu.VMEM((NC // TC, 1, NR), F32),
            pltpu.VMEM((NR // RC, 1, NC), F32),
            pltpu.VMEM((NR // RC, 1, NC), F32),
            pltpu.VMEM((1, NR), F32),
            pltpu.VMEM((COLS, 1, NR), F32),
            pltpu.VMEM((COLS, 1, NR), F32),
            pltpu.VMEM((COLS, 1, NR), F32),
            pltpu.VMEM((ROWS, 4, D), F32),
            pltpu.VMEM((ROWS, 4, D), F32),
            pltpu.VMEM((2, 4, D), F32),
            pltpu.VMEM((COLS, 4, D), F32),
            pltpu.VMEM((ROWS, 4, D), F32),
            pltpu.VMEM((2, 1, NC), F32),
            pltpu.VMEM((ROWS, 1, D), F32),
            pltpu.VMEM((ROWS, 1, D), F32),
            pltpu.VMEM((1, NC), F32),
            pltpu.VMEM((1, D), F32),
            dma, dma, dma, dma((ROWS,)), dma,
            dma((9,)), dma((9,)),
        ],
        compiler_params=pltpu.CompilerParams(
            collective_id=0, has_side_effects=True, vmem_limit_bytes=58 << 20
        ),
    )(source, target, target_potential, prev_moment)
    return pl.pallas_call(
        hand_over,
        out_shape=(
            jax.ShapeDtypeStruct((D, D), F32),
            jax.ShapeDtypeStruct((NR,), F32),
            jax.ShapeDtypeStruct((D,), F32),
        ),
        in_specs=[vmem] * 3,
        out_specs=(vmem,) * 3,
    )(moment, row, col)


def solution(mesh):
    placed = (P(("row", "col"), None), P(("col", "row"), None), P(("col", "row")), P())
    return jax.shard_map(
        per_device,
        mesh=mesh,
        in_specs=placed,
        out_specs=(P(), P("row"), P(("col", "row"))),
        check_vma=False,
    )
```

```python
import math

import jax
import jax.numpy as jnp
from jax import lax
from jax.experimental import pallas as pl
from jax.experimental.pallas import tpu as pltpu
from jax.sharding import PartitionSpec as P

MESH = pl.DeviceIdType.MESH
F32, BF16 = jnp.float32, jnp.bfloat16
D = 128
ROWS = 32
COLS = 8
NR = 1024
NC = 4096
N = 32768
LOG_N = math.log(N)
PAD = 144
TC = NC
RC = NR
CC = NC

NT_DIMS = (((1,), (1,)), ((), ()))
TN_DIMS = (((0,), (0,)), ((), ()))


def split3(value):
    high = value.astype(BF16)
    rest = value - high.astype(F32)
    middle = rest.astype(BF16)
    return high, middle, (rest - middle.astype(F32)).astype(BF16)


def dot_nt(a, b):
    return lax.dot_general(a, b, NT_DIMS, preferred_element_type=F32)


def dot_nn(a, b):
    return jnp.dot(a, b, preferred_element_type=F32)


def kernel(
    source_ref, target_ref, potential_ref, prev_ref,
    moment_ref, row_out_ref, col_out_ref,
    src, tbuf, taug, paug, tile, kernel_tile, frep, chunk_top, col_top, col_mass,
    stage_row, row_in1, row_in2, row_in3,
    mom_stage, mom_in, own_mom, mom_z, mom_all,
    stage_col, col_in, col_in2, col_all, own_col,
    src_send, src_recv, t_send, t_recv, f_send,
    send_sem, recv_sem,
):
    me_r = lax.axis_index("row")
    me_z = lax.axis_index("col")
    core = lax.rem(me_r, 2)
    chip = lax.div(me_r, 2)
    sibling = chip * 2 + (1 - core)

    def row_peer(k):
        return lax.rem(me_r + k, ROWS)

    def z_peer(k):
        return lax.rem(me_z + k, COLS)

    def plane_peer(k):
        return lax.rem(chip + k, ROWS // 2) * 2 + core

    def remote(source, dest, send, recv, row, col):
        return pltpu.make_async_remote_copy(
            src_ref=source, dst_ref=dest, send_sem=send, recv_sem=recv,
            device_id=(row, col), device_id_type=MESH,
        )

    def settle(buffer, sem):
        pltpu.make_async_copy(buffer, buffer, sem).wait()

    barrier = pltpu.get_barrier_semaphore()

    def greet_row(k, _):
        pl.semaphore_signal(barrier, inc=1, device_id=(row_peer(k), me_z), device_id_type=MESH)
        return _

    def greet_z(k, _):
        pl.semaphore_signal(barrier, inc=1, device_id=(me_r, z_peer(k)), device_id_type=MESH)
        return _

    lax.fori_loop(1, ROWS, greet_row, 0, unroll=True)
    lax.fori_loop(1, COLS, greet_z, 0, unroll=True)
    src[me_z] = source_ref[...]
    tbuf[me_r, 0:D] = target_ref[...]
    tbuf[me_r, D:PAD] = jnp.broadcast_to(potential_ref[...].astype(F32).reshape(1, D), (PAD - D, D)).astype(BF16)
    paug[:, D:] = jnp.ones((NR, D), BF16)
    pl.semaphore_wait(barrier, ROWS + COLS - 2)

    def send_source(k, _):
        remote(src.at[me_z], src.at[me_z], src_send, src_recv, me_r, z_peer(k)).start()
        return _

    def send_target(k, _):
        remote(tbuf.at[me_r], tbuf.at[me_r], t_send, t_recv.at[me_r], plane_peer(k), me_z).start()
        return _

    remote(tbuf.at[me_r], tbuf.at[me_r], f_send, t_recv.at[me_r], sibling, me_z).start()
    lax.fori_loop(1, COLS, send_source, 0, unroll=True)
    lax.fori_loop(1, ROWS // 2, send_target, 0, unroll=True)

    def forward(k, _):
        slot = plane_peer(k)
        settle(tbuf.at[slot], t_recv.at[slot])
        remote(tbuf.at[slot], tbuf.at[slot], f_send, t_recv.at[slot], sibling, me_z).start()
        return _

    lax.fori_loop(1, ROWS // 2, forward, 0)

    settle(src.at[pl.ds(0, COLS - 1)], src_recv)
    settle(src.at[pl.ds(0, COLS - 1)], src_send)

    def project(parts):
        rows = src[...].reshape(NR, D)
        total = parts(rows)
        paug[:, 0:D] = (4.0 * total).astype(BF16)

    def project_prev(rows):
        high, middle, low = split3(prev_ref[...])
        return dot_nn(rows, high) + (dot_nn(rows, middle) + dot_nn(rows, low))

    project(project_prev)

    def arrive(k, _):
        slot = lax.rem(chip + k, ROWS // 2) * 2 + (1 - core)
        settle(tbuf.at[slot], t_recv.at[slot])
        return _

    lax.fori_loop(0, ROWS // 2, arrive, 0)
    settle(tbuf.at[pl.ds(0, ROWS // 2 - 1)], t_send)
    settle(tbuf.at[pl.ds(0, ROWS // 2)], f_send)

    eye = lax.broadcasted_iota(jnp.int32, (D, D), 0) == lax.broadcasted_iota(jnp.int32, (D, D), 1)

    def place(k, _):
        block = tbuf[k]
        at = pl.ds(pl.multiple_of(k * D, D), D)
        taug[at, 0:D] = block[0:D]
        taug[at, D:] = jnp.where(eye, block[D : D + 1].astype(F32), 0.0).astype(BF16)
        return _

    lax.fori_loop(0, ROWS, place, 0)

    def row_pass(keep):
        def step(c, carry):
            top, mass = carry
            at = pl.ds(pl.multiple_of(c * TC, TC), TC)
            scores = dot_nt(taug[at, :], paug[...])
            here = jnp.max(scores, axis=0, keepdims=True)
            weights = jnp.exp(scores - here)
            if keep:
                tile[at, :] = weights.astype(BF16)
                chunk_top[c] = here
            new_top = jnp.maximum(top, here)
            mass = mass * jnp.exp(top - new_top) + jnp.sum(weights, axis=0, keepdims=True) * jnp.exp(here - new_top)
            return new_top, mass

        start = (jnp.full((1, NR), -jnp.inf, F32), jnp.zeros((1, NR), F32))
        return lax.fori_loop(0, NC // TC, step, start)

    def send_z(stage, inbox, channel):
        def one(k, _):
            remote(stage, inbox.at[me_z], send_sem.at[channel], recv_sem.at[channel], me_r, z_peer(k)).start()
            return _

        lax.fori_loop(1, COLS, one, 0, unroll=True)
        inbox[me_z] = stage[...]

    def wait_z(inbox, channel):
        settle(inbox.at[pl.ds(0, COLS - 1)], recv_sem.at[channel])
        settle(inbox.at[pl.ds(0, COLS - 1)], send_sem.at[channel])

    def total_lse(inbox):
        values = inbox[...]
        top = jnp.max(values, axis=0)
        return top + jnp.log(jnp.sum(jnp.exp(values - top[None]), axis=0))

    top, mass = row_pass(True)
    stage_row[...] = top + jnp.log(mass)
    send_z(stage_row, row_in1, 0)

    def carry_step(c, total):
        at = pl.ds(pl.multiple_of(c * TC, TC), TC)
        part = lax.dot_general(taug[at, 0:D], tile[at, :], TN_DIMS, preferred_element_type=F32)
        return total + part * jnp.exp(chunk_top[c] - top)

    carried = lax.fori_loop(0, NC // TC, carry_step, jnp.zeros((D, NR), F32))
    wait_z(row_in1, 0)
    carried = carried * (jnp.exp(top - total_lse(row_in1)) / N)
    rows = src[...].reshape(NR, D)
    high, middle, low = split3(carried)
    part_moment = dot_nn(high, rows) + (dot_nn(middle, rows) + dot_nn(low, rows))
    for k in range(ROWS):
        mom_stage[k] = part_moment[4 * k : 4 * k + 4]

    def send_moment(k, _):
        peer = row_peer(k)
        remote(mom_stage.at[peer], mom_in.at[me_r], send_sem.at[1], recv_sem.at[1], peer, me_z).start()
        return _

    lax.fori_loop(1, ROWS, send_moment, 0, unroll=True)
    mom_in[me_r] = mom_stage[me_r]
    settle(mom_in.at[pl.ds(0, ROWS - 1)], recv_sem.at[1])
    settle(mom_in.at[pl.ds(0, ROWS - 1)], send_sem.at[1])
    own_mom[0] = jnp.sum(mom_in[...], axis=0)
    send_z(own_mom.at[0], mom_z, 2)
    wait_z(mom_z, 2)
    own_mom[1] = jnp.sum(mom_z[...], axis=0)

    def share_moment(k, _):
        remote(own_mom.at[1], mom_all.at[me_r], send_sem.at[3], recv_sem.at[3], row_peer(k), me_z).start()
        return _

    lax.fori_loop(1, ROWS, share_moment, 0, unroll=True)
    mom_all[me_r] = own_mom[1]
    settle(mom_all.at[pl.ds(0, ROWS - 1)], recv_sem.at[3])
    settle(mom_all.at[pl.ds(0, ROWS - 1)], send_sem.at[3])
    for k in range(ROWS):
        moment_ref[4 * k : 4 * k + 4, :] = mom_all[k]
    moment_t = moment_ref[...]

    def project_new(block):
        first, second, third = split3(moment_t)
        return dot_nt(block, first) + (dot_nt(block, second) + dot_nt(block, third))

    project(project_new)
    moment_ref[...] = moment_t.T

    top, mass = row_pass(False)
    stage_row[...] = top + jnp.log(mass)
    send_z(stage_row, row_in2, 4)
    wait_z(row_in2, 4)
    first_row = LOG_N - total_lse(row_in2)

    for k in range(NR // D):
        frep[k * D : (k + 1) * D, :] = jnp.broadcast_to(first_row[:, k * D : (k + 1) * D], (D, D)).T

    def col_step(step, _):
        r = lax.div(step, NC // CC)
        c = lax.rem(step, NC // CC)
        rows_at = pl.ds(pl.multiple_of(r * RC, RC), RC)
        cols_at = pl.ds(pl.multiple_of(c * CC, CC), CC)
        shift = frep[rows_at, :]
        scores = dot_nt(paug[rows_at, 0:D], taug[cols_at, 0:D]) + jnp.concatenate([shift] * (CC // D), axis=1)
        here = jnp.max(scores, axis=0, keepdims=True)
        weights = jnp.exp(scores - here)
        kernel_tile[rows_at, cols_at] = weights.astype(BF16)
        col_top[r, :, cols_at] = here
        col_mass[r, :, cols_at] = jnp.sum(weights, axis=0, keepdims=True)
        return _

    lax.fori_loop(0, (NR // RC) * (NC // CC), col_step, 0)
    tops = col_top[...]
    best = jnp.max(tops, axis=0)
    stage_col[0] = best + jnp.log(jnp.sum(col_mass[...] * jnp.exp(tops - best[None]), axis=0))

    def lanes(k):
        return pl.ds(pl.multiple_of(k * D, D), D)

    def scatter_cols(index, inbox, channel):
        def one(k, _):
            peer = row_peer(k)
            remote(
                stage_col.at[index, :, lanes(peer)], inbox.at[me_r],
                send_sem.at[channel], recv_sem.at[channel], peer, me_z,
            ).start()
            return _

        lax.fori_loop(1, ROWS, one, 0, unroll=True)
        inbox[me_r] = stage_col[index, :, lanes(me_r)]
        settle(inbox.at[pl.ds(0, ROWS - 1)], recv_sem.at[channel])
        settle(inbox.at[pl.ds(0, ROWS - 1)], send_sem.at[channel])

    scatter_cols(0, col_in, 5)
    own_col[...] = LOG_N - total_lse(col_in)

    def share_col(k, _):
        remote(own_col, col_all.at[:, lanes(me_r)], send_sem.at[6], recv_sem.at[6], row_peer(k), me_z).start()
        return _

    lax.fori_loop(1, ROWS, share_col, 0, unroll=True)
    col_all[:, lanes(me_r)] = own_col[...]
    settle(col_all.at[:, pl.ds(0, NC - D)], recv_sem.at[6])
    settle(col_all.at[:, pl.ds(0, NC - D)], send_sem.at[6])

    first_col = col_all[...]
    line = lax.broadcasted_iota(jnp.int32, (16, 1), 0)
    lhs = jnp.zeros((16, NC), F32)
    for r in range(NR // RC):
        factor = jnp.exp(first_col + col_top[r])
        col_mass[r] = factor
        for p, piece in enumerate(split3(factor)):
            lhs = jnp.where(line == 3 * r + p, piece.astype(F32), lhs)
    sums = dot_nt(lhs.astype(BF16), kernel_tile[...])
    for r in range(NR // RC):
        at = slice(r * RC, (r + 1) * RC)
        stage_row[:, at] = (
            sums[3 * r : 3 * r + 1, at] + (sums[3 * r + 1 : 3 * r + 2, at] + sums[3 * r + 2 : 3 * r + 3, at])
        )
    send_z(stage_row, row_in3, 7)
    wait_z(row_in3, 7)
    row_sum = jnp.sum(row_in3[...], axis=0)
    row_out_ref[...] = first_row + (LOG_N - jnp.log(row_sum))
    high, middle, low = split3(N / row_sum)
    scale = jnp.where(
        line == 0, high.astype(F32), jnp.where(line == 1, middle.astype(F32), jnp.where(line == 2, low.astype(F32), 0.0))
    ).astype(BF16)
    total = jnp.zeros((1, NC), F32)
    for r in range(NR // RC):
        at = slice(r * RC, (r + 1) * RC)
        part = dot_nn(scale[:, at], kernel_tile[at, :])
        total = total + (part[0:1] + (part[1:2] + part[2:3])) * col_mass[r]
    stage_col[1] = total
    scatter_cols(1, col_in2, 8)
    col_out_ref[...] = own_col[...] + (LOG_N - jnp.log(jnp.sum(col_in2[...], axis=0)))


def hand_over(moment_ref, row_ref, col_ref, moment_out, row_out, col_out):
    moment_out[...] = moment_ref[...]
    row_out[...] = row_ref[...].reshape(NR)
    col_out[...] = col_ref[...].reshape(D)


def per_device(source, target, target_potential, prev_moment):
    vmem = pl.BlockSpec(memory_space=pltpu.VMEM)
    dma = pltpu.SemaphoreType.DMA
    moment, row, col = pl.pallas_call(
        kernel,
        out_shape=(
            jax.ShapeDtypeStruct((D, D), F32),
            jax.ShapeDtypeStruct((1, NR), F32),
            jax.ShapeDtypeStruct((1, D), F32),
        ),
        in_specs=[vmem] * 4,
        out_specs=(vmem,) * 3,
        scratch_shapes=[
            pltpu.VMEM((COLS, D, D), BF16),
            pltpu.VMEM((ROWS, PAD, D), BF16),
            pltpu.VMEM((NC, 2 * D), BF16),
            pltpu.VMEM((NR, 2 * D), BF16),
            pltpu.VMEM((NC, NR), BF16),
            pltpu.VMEM((NR, NC), BF16),
            pltpu.VMEM((NR, D), F32),
            pltpu.VMEM((NC // TC, 1, NR), F32),
            pltpu.VMEM((NR // RC, 1, NC), F32),
            pltpu.VMEM((NR // RC, 1, NC), F32),
            pltpu.VMEM((1, NR), F32),
            pltpu.VMEM((COLS, 1, NR), F32),
            pltpu.VMEM((COLS, 1, NR), F32),
            pltpu.VMEM((COLS, 1, NR), F32),
            pltpu.VMEM((ROWS, 4, D), F32),
            pltpu.VMEM((ROWS, 4, D), F32),
            pltpu.VMEM((2, 4, D), F32),
            pltpu.VMEM((COLS, 4, D), F32),
            pltpu.VMEM((ROWS, 4, D), F32),
            pltpu.VMEM((2, 1, NC), F32),
            pltpu.VMEM((ROWS, 1, D), F32),
            pltpu.VMEM((ROWS, 1, D), F32),
            pltpu.VMEM((1, NC), F32),
            pltpu.VMEM((1, D), F32),
            dma, dma, dma, dma((ROWS,)), dma,
            dma((9,)), dma((9,)),
        ],
        compiler_params=pltpu.CompilerParams(
            collective_id=0, has_side_effects=True, vmem_limit_bytes=58 << 20
        ),
    )(source, target, target_potential, prev_moment)
    return pl.pallas_call(
        hand_over,
        out_shape=(
            jax.ShapeDtypeStruct((D, D), F32),
            jax.ShapeDtypeStruct((NR,), F32),
            jax.ShapeDtypeStruct((D,), F32),
        ),
        in_specs=[vmem] * 3,
        out_specs=(vmem,) * 3,
    )(moment, row, col)


def solution(mesh):
    placed = (P(("row", "col"), None), P(("col", "row"), None), P(("col", "row")), P())
    return jax.shard_map(
        per_device,
        mesh=mesh,
        in_specs=placed,
        out_specs=(P(), P("row"), P(("col", "row"))),
        check_vma=False,
    )
```

```python
import math

import jax
import jax.numpy as jnp
from jax import lax
from jax.experimental import pallas as pl
from jax.experimental.pallas import tpu as pltpu
from jax.sharding import PartitionSpec as P

MESH = pl.DeviceIdType.MESH
F32, BF16 = jnp.float32, jnp.bfloat16
D = 128
ROWS = 32
COLS = 8
NR = 1024
NC = 4096
N = 32768
LOG_N = math.log(N)
PLANE = sorted(((x, y) for x in range(4) for y in range(4)), key=lambda o: -(min(o[0], 4 - o[0]) + min(o[1], 4 - o[1])))
ROW_PEERS = [(x, y, c) for x, y in PLANE for c in (0, 1) if (x, y, c) != (0, 0, 0)]
PLANE_PEERS = [(x, y, 0) for x, y in PLANE if (x, y) != (0, 0)]
Z_PEERS = [4, 3, 5, 2, 6, 1, 7]
PAD = 144
TC = NC
RC = NR
CC = NC

NT_DIMS = (((1,), (1,)), ((), ()))
TN_DIMS = (((0,), (0,)), ((), ()))


def split3(value):
    high = value.astype(BF16)
    rest = value - high.astype(F32)
    middle = rest.astype(BF16)
    return high, middle, (rest - middle.astype(F32)).astype(BF16)


def for_each(start, partners):
    for partner in partners:
        start(partner, 0)


def dot_nt(a, b):
    return lax.dot_general(a, b, NT_DIMS, preferred_element_type=F32)


def dot_nn(a, b):
    return jnp.dot(a, b, preferred_element_type=F32)


def kernel(
    source_ref, target_ref, potential_ref, prev_ref,
    moment_ref, row_out_ref, col_out_ref,
    src, tbuf, taug, paug, tile, kernel_tile, frep, chunk_top, col_top, col_mass,
    stage_row, row_in1, row_in2, row_in3,
    mom_stage, mom_in, own_mom, mom_z, mom_all,
    stage_col, col_in, col_in2, col_all, own_col,
    src_send, src_recv, t_send, t_recv, f_send,
    send_sem, recv_sem,
):
    me_r = lax.axis_index("row")
    me_z = lax.axis_index("col")
    core = lax.rem(me_r, 2)
    chip = lax.div(me_r, 2)
    sibling = chip * 2 + (1 - core)

    chip_x, chip_y = lax.div(chip, 4), lax.rem(chip, 4)

    def row_peer(offset):
        dx, dy, dc = offset
        at = lax.rem(chip_x + dx, 4) * 4 + lax.rem(chip_y + dy, 4)
        return at * 2 + (1 - core if dc else core)

    def z_peer(k):
        return lax.rem(me_z + k, COLS)

    def plane_peer(k):
        return lax.rem(chip + k, ROWS // 2) * 2 + core

    def remote(source, dest, send, recv, row, col):
        return pltpu.make_async_remote_copy(
            src_ref=source, dst_ref=dest, send_sem=send, recv_sem=recv,
            device_id=(row, col), device_id_type=MESH,
        )

    def settle(buffer, sem):
        pltpu.make_async_copy(buffer, buffer, sem).wait()

    barrier = pltpu.get_barrier_semaphore()

    def greet_row(k, _):
        pl.semaphore_signal(barrier, inc=1, device_id=(row_peer(k), me_z), device_id_type=MESH)
        return _

    def greet_z(k, _):
        pl.semaphore_signal(barrier, inc=1, device_id=(me_r, z_peer(k)), device_id_type=MESH)
        return _

    for_each(greet_row, ROW_PEERS)
    for_each(greet_z, Z_PEERS)
    src[me_z] = source_ref[...]
    tbuf[me_r, 0:D] = target_ref[...]
    tbuf[me_r, D:PAD] = jnp.broadcast_to(potential_ref[...].astype(F32).reshape(1, D), (PAD - D, D)).astype(BF16)
    paug[:, D:] = jnp.ones((NR, D), BF16)
    pl.semaphore_wait(barrier, ROWS + COLS - 2)

    def send_source(k, _):
        remote(src.at[me_z], src.at[me_z], src_send, src_recv, me_r, z_peer(k)).start()
        return _

    def send_target(k, _):
        remote(tbuf.at[me_r], tbuf.at[me_r], t_send, t_recv.at[me_r], row_peer(k), me_z).start()
        return _

    remote(tbuf.at[me_r], tbuf.at[me_r], f_send, t_recv.at[me_r], sibling, me_z).start()
    for_each(send_source, Z_PEERS)
    for_each(send_target, PLANE_PEERS)

    eye = lax.broadcasted_iota(jnp.int32, (D, D), 0) == lax.broadcasted_iota(jnp.int32, (D, D), 1)

    def place(slot):
        block = tbuf[slot]
        at = pl.ds(pl.multiple_of(slot * D, D), D)
        taug[at, 0:D] = block[0:D]
        taug[at, D:] = jnp.where(eye, block[D : D + 1].astype(F32), 0.0).astype(BF16)

    place(me_r)

    def forward(k, _):
        slot = plane_peer(k)
        settle(tbuf.at[slot], t_recv.at[slot])
        remote(tbuf.at[slot], tbuf.at[slot], f_send, t_recv.at[slot], sibling, me_z).start()
        place(slot)
        return _

    lax.fori_loop(1, ROWS // 2, forward, 0)

    settle(src.at[pl.ds(0, COLS - 1)], src_recv)
    settle(src.at[pl.ds(0, COLS - 1)], src_send)

    def project(parts):
        rows = src[...].reshape(NR, D)
        total = parts(rows)
        paug[:, 0:D] = (4.0 * total).astype(BF16)

    def project_prev(rows):
        wide = dot_nn(rows, jnp.concatenate(split3(prev_ref[...]), axis=1))
        return wide[:, 0:D] + (wide[:, D : 2 * D] + wide[:, 2 * D :])

    project(project_prev)

    def arrive(k, _):
        slot = lax.rem(chip + k, ROWS // 2) * 2 + (1 - core)
        settle(tbuf.at[slot], t_recv.at[slot])
        place(slot)
        return _

    lax.fori_loop(0, ROWS // 2, arrive, 0)
    settle(tbuf.at[pl.ds(0, ROWS // 2 - 1)], t_send)
    settle(tbuf.at[pl.ds(0, ROWS // 2)], f_send)

    def row_pass(keep):
        def step(c, carry):
            top, mass = carry
            at = pl.ds(pl.multiple_of(c * TC, TC), TC)
            scores = dot_nt(taug[at, :], paug[...])
            here = jnp.max(scores, axis=0, keepdims=True)
            weights = jnp.exp(scores - here)
            if keep:
                tile[at, :] = weights.astype(BF16)
                chunk_top[c] = here
            new_top = jnp.maximum(top, here)
            mass = mass * jnp.exp(top - new_top) + jnp.sum(weights, axis=0, keepdims=True) * jnp.exp(here - new_top)
            return new_top, mass

        start = (jnp.full((1, NR), -jnp.inf, F32), jnp.zeros((1, NR), F32))
        return lax.fori_loop(0, NC // TC, step, start)

    def send_z(stage, inbox, channel):
        def one(k, _):
            remote(stage, inbox.at[me_z], send_sem.at[channel], recv_sem.at[channel], me_r, z_peer(k)).start()
            return _

        for_each(one, Z_PEERS)
        inbox[me_z] = stage[...]

    def wait_z(inbox, channel):
        settle(inbox.at[pl.ds(0, COLS - 1)], recv_sem.at[channel])
        settle(inbox.at[pl.ds(0, COLS - 1)], send_sem.at[channel])

    def total_lse(inbox):
        values = inbox[...]
        top = jnp.max(values, axis=0)
        return top + jnp.log(jnp.sum(jnp.exp(values - top[None]), axis=0))

    top, mass = row_pass(True)
    stage_row[...] = top + jnp.log(mass)
    send_z(stage_row, row_in1, 0)

    def carry_step(c, total):
        at = pl.ds(pl.multiple_of(c * TC, TC), TC)
        part = lax.dot_general(taug[at, 0:D], tile[at, :], TN_DIMS, preferred_element_type=F32)
        return total + part * jnp.exp(chunk_top[c] - top)

    carried = lax.fori_loop(0, NC // TC, carry_step, jnp.zeros((D, NR), F32))
    wait_z(row_in1, 0)
    carried = carried * (jnp.exp(top - total_lse(row_in1)) / N)
    rows = src[...].reshape(NR, D)
    tall = dot_nn(jnp.concatenate(split3(carried), axis=0), rows)
    part_moment = tall[0:D] + (tall[D : 2 * D] + tall[2 * D :])
    for k in range(ROWS):
        mom_stage[k] = part_moment[4 * k : 4 * k + 4]

    def send_moment(k, _):
        peer = row_peer(k)
        remote(mom_stage.at[peer], mom_in.at[me_r], send_sem.at[1], recv_sem.at[1], peer, me_z).start()
        return _

    for_each(send_moment, ROW_PEERS)
    mom_in[me_r] = mom_stage[me_r]
    settle(mom_in.at[pl.ds(0, ROWS - 1)], recv_sem.at[1])
    settle(mom_in.at[pl.ds(0, ROWS - 1)], send_sem.at[1])
    own_mom[0] = jnp.sum(mom_in[...], axis=0)
    send_z(own_mom.at[0], mom_z, 2)
    wait_z(mom_z, 2)
    own_mom[1] = jnp.sum(mom_z[...], axis=0)

    def share_moment(k, _):
        remote(own_mom.at[1], mom_all.at[me_r], send_sem.at[3], recv_sem.at[3], row_peer(k), me_z).start()
        return _

    for_each(share_moment, ROW_PEERS)
    mom_all[me_r] = own_mom[1]
    settle(mom_all.at[pl.ds(0, ROWS - 1)], recv_sem.at[3])
    settle(mom_all.at[pl.ds(0, ROWS - 1)], send_sem.at[3])
    for k in range(ROWS):
        moment_ref[4 * k : 4 * k + 4, :] = mom_all[k]
    moment_t = moment_ref[...]

    def project_new(block):
        wide = dot_nt(block, jnp.concatenate(split3(moment_t), axis=0))
        return wide[:, 0:D] + (wide[:, D : 2 * D] + wide[:, 2 * D :])

    project(project_new)
    moment_ref[...] = moment_t.T

    top, mass = row_pass(False)
    stage_row[...] = top + jnp.log(mass)
    send_z(stage_row, row_in2, 4)
    wait_z(row_in2, 4)
    first_row = LOG_N - total_lse(row_in2)

    for k in range(NR // D):
        frep[k * D : (k + 1) * D, :] = jnp.broadcast_to(first_row[:, k * D : (k + 1) * D], (D, D)).T

    def col_step(step, _):
        r = lax.div(step, NC // CC)
        c = lax.rem(step, NC // CC)
        rows_at = pl.ds(pl.multiple_of(r * RC, RC), RC)
        cols_at = pl.ds(pl.multiple_of(c * CC, CC), CC)
        shift = frep[rows_at, :]
        scores = dot_nt(paug[rows_at, 0:D], taug[cols_at, 0:D]) + jnp.concatenate([shift] * (CC // D), axis=1)
        here = jnp.max(scores, axis=0, keepdims=True)
        weights = jnp.exp(scores - here)
        kernel_tile[rows_at, cols_at] = weights.astype(BF16)
        col_top[r, :, cols_at] = here
        col_mass[r, :, cols_at] = jnp.sum(weights, axis=0, keepdims=True)
        return _

    lax.fori_loop(0, (NR // RC) * (NC // CC), col_step, 0)
    tops = col_top[...]
    best = jnp.max(tops, axis=0)
    stage_col[0] = best + jnp.log(jnp.sum(col_mass[...] * jnp.exp(tops - best[None]), axis=0))

    def lanes(k):
        return pl.ds(pl.multiple_of(k * D, D), D)

    def scatter_cols(index, inbox, channel):
        def one(k, _):
            peer = row_peer(k)
            remote(
                stage_col.at[index, :, lanes(peer)], inbox.at[me_r],
                send_sem.at[channel], recv_sem.at[channel], peer, me_z,
            ).start()
            return _

        for_each(one, ROW_PEERS)
        inbox[me_r] = stage_col[index, :, lanes(me_r)]
        settle(inbox.at[pl.ds(0, ROWS - 1)], recv_sem.at[channel])
        settle(inbox.at[pl.ds(0, ROWS - 1)], send_sem.at[channel])

    scatter_cols(0, col_in, 5)
    own_col[...] = LOG_N - total_lse(col_in)

    def share_col(k, _):
        remote(own_col, col_all.at[:, lanes(me_r)], send_sem.at[6], recv_sem.at[6], row_peer(k), me_z).start()
        return _

    for_each(share_col, ROW_PEERS)
    col_all[:, lanes(me_r)] = own_col[...]
    settle(col_all.at[:, pl.ds(0, NC - D)], recv_sem.at[6])
    settle(col_all.at[:, pl.ds(0, NC - D)], send_sem.at[6])

    first_col = col_all[...]
    line = lax.broadcasted_iota(jnp.int32, (16, 1), 0)
    lhs = jnp.zeros((16, NC), F32)
    for r in range(NR // RC):
        factor = jnp.exp(first_col + col_top[r])
        col_mass[r] = factor
        for p, piece in enumerate(split3(factor)):
            lhs = jnp.where(line == 3 * r + p, piece.astype(F32), lhs)
    sums = dot_nt(lhs.astype(BF16), kernel_tile[...])
    for r in range(NR // RC):
        at = slice(r * RC, (r + 1) * RC)
        stage_row[:, at] = (
            sums[3 * r : 3 * r + 1, at] + (sums[3 * r + 1 : 3 * r + 2, at] + sums[3 * r + 2 : 3 * r + 3, at])
        )
    send_z(stage_row, row_in3, 7)
    wait_z(row_in3, 7)
    row_sum = jnp.sum(row_in3[...], axis=0)
    row_out_ref[...] = first_row + (LOG_N - jnp.log(row_sum))
    high, middle, low = split3(N / row_sum)
    scale = jnp.where(
        line == 0, high.astype(F32), jnp.where(line == 1, middle.astype(F32), jnp.where(line == 2, low.astype(F32), 0.0))
    ).astype(BF16)
    total = jnp.zeros((1, NC), F32)
    for r in range(NR // RC):
        at = slice(r * RC, (r + 1) * RC)
        part = dot_nn(scale[:, at], kernel_tile[at, :])
        total = total + (part[0:1] + (part[1:2] + part[2:3])) * col_mass[r]
    stage_col[1] = total
    scatter_cols(1, col_in2, 8)
    col_out_ref[...] = own_col[...] + (LOG_N - jnp.log(jnp.sum(col_in2[...], axis=0)))


def hand_over(moment_ref, row_ref, col_ref, moment_out, row_out, col_out):
    moment_out[...] = moment_ref[...]
    row_out[...] = row_ref[...].reshape(NR)
    col_out[...] = col_ref[...].reshape(D)


def per_device(source, target, target_potential, prev_moment):
    vmem = pl.BlockSpec(memory_space=pltpu.VMEM)
    dma = pltpu.SemaphoreType.DMA
    moment, row, col = pl.pallas_call(
        kernel,
        out_shape=(
            jax.ShapeDtypeStruct((D, D), F32),
            jax.ShapeDtypeStruct((1, NR), F32),
            jax.ShapeDtypeStruct((1, D), F32),
        ),
        in_specs=[vmem] * 4,
        out_specs=(vmem,) * 3,
        scratch_shapes=[
            pltpu.VMEM((COLS, D, D), BF16),
            pltpu.VMEM((ROWS, PAD, D), BF16),
            pltpu.VMEM((NC, 2 * D), BF16),
            pltpu.VMEM((NR, 2 * D), BF16),
            pltpu.VMEM((NC, NR), BF16),
            pltpu.VMEM((NR, NC), BF16),
            pltpu.VMEM((NR, D), F32),
            pltpu.VMEM((NC // TC, 1, NR), F32),
            pltpu.VMEM((NR // RC, 1, NC), F32),
            pltpu.VMEM((NR // RC, 1, NC), F32),
            pltpu.VMEM((1, NR), F32),
            pltpu.VMEM((COLS, 1, NR), F32),
            pltpu.VMEM((COLS, 1, NR), F32),
            pltpu.VMEM((COLS, 1, NR), F32),
            pltpu.VMEM((ROWS, 4, D), F32),
            pltpu.VMEM((ROWS, 4, D), F32),
            pltpu.VMEM((2, 4, D), F32),
            pltpu.VMEM((COLS, 4, D), F32),
            pltpu.VMEM((ROWS, 4, D), F32),
            pltpu.VMEM((2, 1, NC), F32),
            pltpu.VMEM((ROWS, 1, D), F32),
            pltpu.VMEM((ROWS, 1, D), F32),
            pltpu.VMEM((1, NC), F32),
            pltpu.VMEM((1, D), F32),
            dma, dma, dma, dma((ROWS,)), dma,
            dma((9,)), dma((9,)),
        ],
        compiler_params=pltpu.CompilerParams(
            collective_id=0, has_side_effects=True, vmem_limit_bytes=58 << 20
        ),
    )(source, target, target_potential, prev_moment)
    return pl.pallas_call(
        hand_over,
        out_shape=(
            jax.ShapeDtypeStruct((D, D), F32),
            jax.ShapeDtypeStruct((NR,), F32),
            jax.ShapeDtypeStruct((D,), F32),
        ),
        in_specs=[vmem] * 3,
        out_specs=(vmem,) * 3,
    )(moment, row, col)


def solution(mesh):
    placed = (P(("row", "col"), None), P(("col", "row"), None), P(("col", "row")), P())
    return jax.shard_map(
        per_device,
        mesh=mesh,
        in_specs=placed,
        out_specs=(P(), P("row"), P(("col", "row"))),
        check_vma=False,
    )
```

```python
import math

import jax
import jax.numpy as jnp
from jax import lax
from jax.experimental import pallas as pl
from jax.experimental.pallas import tpu as pltpu
from jax.sharding import PartitionSpec as P

MESH = pl.DeviceIdType.MESH
F32, BF16 = jnp.float32, jnp.bfloat16
D = 128
ROWS = 32
COLS = 8
NR = 1024
NC = 4096
N = 32768
LOG_N = math.log(N)
PLANE = sorted(((x, y) for x in range(4) for y in range(4)), key=lambda o: -(min(o[0], 4 - o[0]) + min(o[1], 4 - o[1])))
ROW_PEERS = [(x, y, c) for x, y in PLANE for c in (0, 1) if (x, y, c) != (0, 0, 0)]
PLANE_PEERS = [(x, y, 0) for x, y in PLANE if (x, y) != (0, 0)]
Z_PEERS = [4, 3, 5, 2, 6, 1, 7]
PAD = 144
TC = NC
RC = NR
CC = NC

NT_DIMS = (((1,), (1,)), ((), ()))
TN_DIMS = (((0,), (0,)), ((), ()))


def split3(value):
    high = value.astype(BF16)
    rest = value - high.astype(F32)
    middle = rest.astype(BF16)
    return high, middle, (rest - middle.astype(F32)).astype(BF16)


def for_each(start, partners):
    for partner in partners:
        start(partner, 0)


def dot_nt(a, b):
    return lax.dot_general(a, b, NT_DIMS, preferred_element_type=F32)


def dot_nn(a, b):
    return jnp.dot(a, b, preferred_element_type=F32)


def kernel(
    source_ref, target_ref, potential_ref, prev_ref,
    moment_ref, row_out_ref, col_out_ref,
    src, tbuf, taug, paug, tile, kernel_tile, frep, chunk_top, col_top, col_mass,
    stage_row, row_in1, row_in2, row_in3,
    mom_stage, mom_in, own_mom, mom_z, mom_all,
    stage_col, col_in, col_in2, col_all, own_col,
    src_send, src_recv, t_send, t_recv, f_send,
    send_sem, recv_sem,
):
    me_r = lax.axis_index("row")
    me_z = lax.axis_index("col")
    core = lax.rem(me_r, 2)
    chip = lax.div(me_r, 2)
    sibling = chip * 2 + (1 - core)

    chip_x, chip_y = lax.div(chip, 4), lax.rem(chip, 4)

    def row_peer(offset):
        dx, dy, dc = offset
        at = lax.rem(chip_x + dx, 4) * 4 + lax.rem(chip_y + dy, 4)
        return at * 2 + (1 - core if dc else core)

    def z_peer(k):
        return lax.rem(me_z + k, COLS)

    def remote(source, dest, send, recv, row, col):
        return pltpu.make_async_remote_copy(
            src_ref=source, dst_ref=dest, send_sem=send, recv_sem=recv,
            device_id=(row, col), device_id_type=MESH,
        )

    def settle(buffer, sem):
        pltpu.make_async_copy(buffer, buffer, sem).wait()

    barrier = pltpu.get_barrier_semaphore()

    def greet_row(k, _):
        pl.semaphore_signal(barrier, inc=1, device_id=(row_peer(k), me_z), device_id_type=MESH)
        return _

    def greet_z(k, _):
        pl.semaphore_signal(barrier, inc=1, device_id=(me_r, z_peer(k)), device_id_type=MESH)
        return _

    for_each(greet_row, ROW_PEERS)
    for_each(greet_z, Z_PEERS)
    src[me_z] = source_ref[...]
    tbuf[me_r, 0:D] = target_ref[...]
    tbuf[me_r, D:PAD] = jnp.broadcast_to(potential_ref[...].astype(F32).reshape(1, D), (PAD - D, D)).astype(BF16)
    paug[:, D:] = jnp.ones((NR, D), BF16)
    pl.semaphore_wait(barrier, ROWS + COLS - 2)

    def send_source(k, _):
        remote(src.at[me_z], src.at[me_z], src_send, src_recv, me_r, z_peer(k)).start()
        return _

    def send_target(k, _):
        remote(tbuf.at[me_r], tbuf.at[me_r], t_send, t_recv.at[me_r], row_peer(k), me_z).start()
        return _

    remote(tbuf.at[me_r], tbuf.at[me_r], f_send, t_recv.at[me_r], sibling, me_z).start()
    for_each(send_source, Z_PEERS)
    for_each(send_target, PLANE_PEERS)

    eye = lax.broadcasted_iota(jnp.int32, (D, D), 0) == lax.broadcasted_iota(jnp.int32, (D, D), 1)

    def place(slot):
        block = tbuf[slot]
        at = pl.ds(pl.multiple_of(slot * D, D), D)
        taug[at, 0:D] = block[0:D]
        taug[at, D:] = jnp.where(eye, block[D : D + 1].astype(F32), 0.0).astype(BF16)

    place(me_r)

    def forward(k, _):
        slot = row_peer(k)
        settle(tbuf.at[slot], t_recv.at[slot])
        remote(tbuf.at[slot], tbuf.at[slot], f_send, t_recv.at[slot], sibling, me_z).start()
        place(slot)
        return _

    for_each(forward, PLANE_PEERS[::-1])

    settle(src.at[pl.ds(0, COLS - 1)], src_recv)
    settle(src.at[pl.ds(0, COLS - 1)], src_send)

    def project(parts):
        rows = src[...].reshape(NR, D)
        total = parts(rows)
        paug[:, 0:D] = (4.0 * total).astype(BF16)

    def project_prev(rows):
        wide = dot_nn(rows, jnp.concatenate(split3(prev_ref[...]), axis=1))
        return wide[:, 0:D] + (wide[:, D : 2 * D] + wide[:, 2 * D :])

    project(project_prev)

    def arrive(k, _):
        slot = row_peer(k)
        settle(tbuf.at[slot], t_recv.at[slot])
        place(slot)
        return _

    for_each(arrive, [(x, y, 1) for x, y in PLANE[::-1]])
    settle(tbuf.at[pl.ds(0, ROWS // 2 - 1)], t_send)
    settle(tbuf.at[pl.ds(0, ROWS // 2)], f_send)

    def row_pass(keep):
        def step(c, carry):
            top, mass = carry
            at = pl.ds(pl.multiple_of(c * TC, TC), TC)
            scores = dot_nt(taug[at, :], paug[...])
            here = jnp.max(scores, axis=0, keepdims=True)
            weights = jnp.exp(scores - here)
            if keep:
                tile[at, :] = weights.astype(BF16)
                chunk_top[c] = here
            new_top = jnp.maximum(top, here)
            mass = mass * jnp.exp(top - new_top) + jnp.sum(weights, axis=0, keepdims=True) * jnp.exp(here - new_top)
            return new_top, mass

        start = (jnp.full((1, NR), -jnp.inf, F32), jnp.zeros((1, NR), F32))
        return lax.fori_loop(0, NC // TC, step, start)

    def send_z(stage, inbox, channel):
        def one(k, _):
            remote(stage, inbox.at[me_z], send_sem.at[channel], recv_sem.at[channel], me_r, z_peer(k)).start()
            return _

        for_each(one, Z_PEERS)
        inbox[me_z] = stage[...]

    def wait_z(inbox, channel):
        settle(inbox.at[pl.ds(0, COLS - 1)], recv_sem.at[channel])
        settle(inbox.at[pl.ds(0, COLS - 1)], send_sem.at[channel])

    def total_lse(inbox):
        values = inbox[...]
        top = jnp.max(values, axis=0)
        return top + jnp.log(jnp.sum(jnp.exp(values - top[None]), axis=0))

    top, mass = row_pass(True)
    stage_row[...] = top + jnp.log(mass)
    send_z(stage_row, row_in1, 0)

    def carry_step(c, total):
        at = pl.ds(pl.multiple_of(c * TC, TC), TC)
        part = lax.dot_general(taug[at, 0:D], tile[at, :], TN_DIMS, preferred_element_type=F32)
        return total + part * jnp.exp(chunk_top[c] - top)

    carried = lax.fori_loop(0, NC // TC, carry_step, jnp.zeros((D, NR), F32))
    wait_z(row_in1, 0)
    carried = carried * (jnp.exp(top - total_lse(row_in1)) / N)
    rows = src[...].reshape(NR, D)
    tall = dot_nn(jnp.concatenate(split3(carried), axis=0), rows)
    part_moment = tall[0:D] + (tall[D : 2 * D] + tall[2 * D :])
    for k in range(ROWS):
        mom_stage[k] = part_moment[4 * k : 4 * k + 4]

    def send_moment(k, _):
        peer = row_peer(k)
        remote(mom_stage.at[peer], mom_in.at[me_r], send_sem.at[1], recv_sem.at[1], peer, me_z).start()
        return _

    for_each(send_moment, ROW_PEERS)
    mom_in[me_r] = mom_stage[me_r]
    settle(mom_in.at[pl.ds(0, ROWS - 1)], recv_sem.at[1])
    settle(mom_in.at[pl.ds(0, ROWS - 1)], send_sem.at[1])
    own_mom[0] = jnp.sum(mom_in[...], axis=0)
    send_z(own_mom.at[0], mom_z, 2)
    wait_z(mom_z, 2)
    own_mom[1] = jnp.sum(mom_z[...], axis=0)

    def share_moment(k, _):
        remote(own_mom.at[1], mom_all.at[me_r], send_sem.at[3], recv_sem.at[3], row_peer(k), me_z).start()
        return _

    for_each(share_moment, ROW_PEERS)
    mom_all[me_r] = own_mom[1]
    settle(mom_all.at[pl.ds(0, ROWS - 1)], recv_sem.at[3])
    settle(mom_all.at[pl.ds(0, ROWS - 1)], send_sem.at[3])
    for k in range(ROWS):
        moment_ref[4 * k : 4 * k + 4, :] = mom_all[k]
    moment_t = moment_ref[...]

    def project_new(block):
        wide = dot_nt(block, jnp.concatenate(split3(moment_t), axis=0))
        return wide[:, 0:D] + (wide[:, D : 2 * D] + wide[:, 2 * D :])

    project(project_new)
    moment_ref[...] = moment_t.T

    top, mass = row_pass(False)
    stage_row[...] = top + jnp.log(mass)
    send_z(stage_row, row_in2, 4)
    wait_z(row_in2, 4)
    first_row = LOG_N - total_lse(row_in2)

    for k in range(NR // D):
        frep[k * D : (k + 1) * D, :] = jnp.broadcast_to(first_row[:, k * D : (k + 1) * D], (D, D)).T

    def col_step(step, _):
        r = lax.div(step, NC // CC)
        c = lax.rem(step, NC // CC)
        rows_at = pl.ds(pl.multiple_of(r * RC, RC), RC)
        cols_at = pl.ds(pl.multiple_of(c * CC, CC), CC)
        shift = frep[rows_at, :]
        scores = dot_nt(paug[rows_at, 0:D], taug[cols_at, 0:D]) + jnp.concatenate([shift] * (CC // D), axis=1)
        here = jnp.max(scores, axis=0, keepdims=True)
        weights = jnp.exp(scores - here)
        kernel_tile[rows_at, cols_at] = weights.astype(BF16)
        col_top[r, :, cols_at] = here
        col_mass[r, :, cols_at] = jnp.sum(weights, axis=0, keepdims=True)
        return _

    lax.fori_loop(0, (NR // RC) * (NC // CC), col_step, 0)
    stage_col[0] = col_top[0] + jnp.log(col_mass[0])

    def lanes(k):
        return pl.ds(pl.multiple_of(k * D, D), D)

    def scatter_cols(index, inbox, channel):
        def one(k, _):
            peer = row_peer(k)
            remote(
                stage_col.at[index, :, lanes(peer)], inbox.at[me_r],
                send_sem.at[channel], recv_sem.at[channel], peer, me_z,
            ).start()
            return _

        for_each(one, ROW_PEERS)
        inbox[me_r] = stage_col[index, :, lanes(me_r)]
        settle(inbox.at[pl.ds(0, ROWS - 1)], recv_sem.at[channel])
        settle(inbox.at[pl.ds(0, ROWS - 1)], send_sem.at[channel])

    scatter_cols(0, col_in, 5)
    own_col[...] = LOG_N - total_lse(col_in)

    def share_col(k, _):
        remote(own_col, col_all.at[:, lanes(me_r)], send_sem.at[6], recv_sem.at[6], row_peer(k), me_z).start()
        return _

    for_each(share_col, ROW_PEERS)
    col_all[:, lanes(me_r)] = own_col[...]
    settle(col_all.at[:, pl.ds(0, NC - D)], recv_sem.at[6])
    settle(col_all.at[:, pl.ds(0, NC - D)], send_sem.at[6])

    first_col = col_all[...]
    line = lax.broadcasted_iota(jnp.int32, (16, 1), 0)
    lhs = jnp.zeros((16, NC), F32)
    for r in range(NR // RC):
        factor = jnp.exp(first_col + col_top[r])
        col_mass[r] = factor
        for p, piece in enumerate(split3(factor)):
            lhs = jnp.where(line == 3 * r + p, piece.astype(F32), lhs)
    sums = dot_nt(lhs.astype(BF16), kernel_tile[...])
    for r in range(NR // RC):
        at = slice(r * RC, (r + 1) * RC)
        stage_row[:, at] = (
            sums[3 * r : 3 * r + 1, at] + (sums[3 * r + 1 : 3 * r + 2, at] + sums[3 * r + 2 : 3 * r + 3, at])
        )
    send_z(stage_row, row_in3, 7)
    wait_z(row_in3, 7)
    row_sum = jnp.sum(row_in3[...], axis=0)
    row_out_ref[...] = first_row + (LOG_N - jnp.log(row_sum))
    high, middle, low = split3(N / row_sum)
    scale = jnp.where(
        line == 0, high.astype(F32), jnp.where(line == 1, middle.astype(F32), jnp.where(line == 2, low.astype(F32), 0.0))
    ).astype(BF16)
    total = jnp.zeros((1, NC), F32)
    for r in range(NR // RC):
        at = slice(r * RC, (r + 1) * RC)
        part = dot_nn(scale[:, at], kernel_tile[at, :])
        total = total + (part[0:1] + (part[1:2] + part[2:3])) * col_mass[r]
    stage_col[1] = total
    scatter_cols(1, col_in2, 8)
    col_out_ref[...] = own_col[...] + (LOG_N - jnp.log(jnp.sum(col_in2[...], axis=0)))


def hand_over(moment_ref, row_ref, col_ref, moment_out, row_out, col_out):
    moment_out[...] = moment_ref[...]
    row_out[...] = row_ref[...].reshape(NR)
    col_out[...] = col_ref[...].reshape(D)


def per_device(source, target, target_potential, prev_moment):
    vmem = pl.BlockSpec(memory_space=pltpu.VMEM)
    dma = pltpu.SemaphoreType.DMA
    moment, row, col = pl.pallas_call(
        kernel,
        out_shape=(
            jax.ShapeDtypeStruct((D, D), F32),
            jax.ShapeDtypeStruct((1, NR), F32),
            jax.ShapeDtypeStruct((1, D), F32),
        ),
        in_specs=[vmem] * 4,
        out_specs=(vmem,) * 3,
        scratch_shapes=[
            pltpu.VMEM((COLS, D, D), BF16),
            pltpu.VMEM((ROWS, PAD, D), BF16),
            pltpu.VMEM((NC, 2 * D), BF16),
            pltpu.VMEM((NR, 2 * D), BF16),
            pltpu.VMEM((NC, NR), BF16),
            pltpu.VMEM((NR, NC), BF16),
            pltpu.VMEM((NR, D), F32),
            pltpu.VMEM((NC // TC, 1, NR), F32),
            pltpu.VMEM((NR // RC, 1, NC), F32),
            pltpu.VMEM((NR // RC, 1, NC), F32),
            pltpu.VMEM((1, NR), F32),
            pltpu.VMEM((COLS, 1, NR), F32),
            pltpu.VMEM((COLS, 1, NR), F32),
            pltpu.VMEM((COLS, 1, NR), F32),
            pltpu.VMEM((ROWS, 4, D), F32),
            pltpu.VMEM((ROWS, 4, D), F32),
            pltpu.VMEM((2, 4, D), F32),
            pltpu.VMEM((COLS, 4, D), F32),
            pltpu.VMEM((ROWS, 4, D), F32),
            pltpu.VMEM((2, 1, NC), F32),
            pltpu.VMEM((ROWS, 1, D), F32),
            pltpu.VMEM((ROWS, 1, D), F32),
            pltpu.VMEM((1, NC), F32),
            pltpu.VMEM((1, D), F32),
            dma, dma, dma, dma((ROWS,)), dma,
            dma((9,)), dma((9,)),
        ],
        compiler_params=pltpu.CompilerParams(
            collective_id=0, has_side_effects=True, vmem_limit_bytes=58 << 20
        ),
    )(source, target, target_potential, prev_moment)
    return pl.pallas_call(
        hand_over,
        out_shape=(
            jax.ShapeDtypeStruct((D, D), F32),
            jax.ShapeDtypeStruct((NR,), F32),
            jax.ShapeDtypeStruct((D,), F32),
        ),
        in_specs=[vmem] * 3,
        out_specs=(vmem,) * 3,
    )(moment, row, col)


def solution(mesh):
    placed = (P(("row", "col"), None), P(("col", "row"), None), P(("col", "row")), P())
    return jax.shard_map(
        per_device,
        mesh=mesh,
        in_specs=placed,
        out_specs=(P(), P("row"), P(("col", "row"))),
        check_vma=False,
    )
```
